768 devices in a mesh: dp: 24 (over z, core), node: 8 (over y), chip: 4 (over x).
Axes of the slice: x: 4, y: 8, z: 12, core: 2. Of those that a mesh axis runs over, the one named last changes fastest.
Arguments:
- tokens: bfloat16 [49152, 2048], P(('dp', 'node', 'chip')), parts along dimension 0, may hold values from -6 to 6
- expert_ids: int32 [49152, 8], P(('dp', 'node', 'chip')), parts along dimension 0, may hold values from 0 to 31, as said below
- gate_fixed: int32 [49152, 8], P(('dp', 'node', 'chip')), parts along dimension 0, may hold values from 1 to 255
- w_gate: bfloat16 [32, 2048, 768], P(('node', 'chip')), may hold values from -0.125 to 0.125
- w_up: bfloat16 [32, 2048, 768], P(('node', 'chip')), may hold values from -0.125 to 0.125
- w_down: bfloat16 [32, 768, 2048], P(('node', 'chip')), may hold values from -0.21875 to 0.21875
Outputs:
- mixed: bfloat16 [49152, 2048], P(('dp', 'node', 'chip')), parts along dimension 0
The draws below stay inside these ranges and needn't reach their ends.
There are 24 independent parts, one for each index of `dp`. The reference program is written for one: setup_inputs(seed, part) draws one part's arguments, and reference() takes and returns one part's arrays. A program takes and returns all parts, laid end to end along the dimension named above; an argument that names none is the same for every part. Nothing has to cross between parts.
Inputs may be any that keep to these rules, and one draw needn't show every extreme that they name: `expert_ids`: each row names 8 different experts, all within at most 4 groups, expert e belonging to group e // 4. One expert is named by 16 or more tokens of every block of 64 tokens.
All inputs are finite; a program needn't handle non-finite values.
Results may differ from the reference program's by a relative error of at most 0.0057.
Values may be sent and summed in bfloat16 or wider, within the bound.
No kernel may reach another device: no remote copies, remote signals or barrier semaphores. Data moves between devices by JAX's collectives and lax.ppermute only.
A program may use at most 64 MiB of HBM per device.

```python
import jax
import jax.numpy as jnp
from jax import lax

D = 2048
FF = 768
TOP = 8
TOK_DEV = 64
NODES = 8
GROUP = 4
DEVS = 32
EXPERTS = 32
TOKENS = 2048
CAP = 16
NODES_MAX = 4


def draw_expert_ids(key, part):
    key = jax.random.fold_in(key, 11)
    key_hot, key_need, key_node, key_expert = jax.random.split(key, 4)
    hot_expert = jax.random.randint(key_hot, (), 0, EXPERTS)
    hot_group = hot_expert // GROUP
    local_index = jnp.arange(TOKENS, dtype=jnp.int32) % TOK_DEV
    need_hot = (local_index < CAP) | (jax.random.randint(key_need, (TOKENS,), 0, 2) == 1)
    group_range = jnp.arange(NODES, dtype=jnp.int32)
    group_score = jax.random.randint(key_node, (TOKENS, NODES), 0, 1 << 20) * NODES + group_range[None, :]
    group_score = jnp.where(need_hot[:, None] & (group_range[None, :] == hot_group), 1 << 30, group_score)
    chosen_values, chosen = lax.top_k(group_score, NODES_MAX)
    allowed = jnp.any(chosen[:, :, None] == group_range[None, None, :], axis=1)
    expert_range = jnp.arange(EXPERTS, dtype=jnp.int32)
    allowed_expert = jnp.take(allowed, expert_range // GROUP, axis=1)
    expert_score = jax.random.randint(key_expert, (TOKENS, EXPERTS), 0, 1 << 20) * EXPERTS + expert_range[None, :]
    expert_score = jnp.where(allowed_expert, expert_score, expert_score - (1 << 29))
    expert_score = jnp.where(need_hot[:, None] & (expert_range[None, :] == hot_expert), 1 << 30, expert_score)
    score_values, picked = lax.top_k(expert_score, TOP)
    return picked.astype(jnp.int32)


def with_ends(array, stream_key, low, largest):
    longest = array.shape.index(max(array.shape))
    spots = []
    for shift in (0, 1):
        where = [jax.random.randint(jax.random.fold_in(stream_key, axis), (), 0, length) for axis, length in enumerate(array.shape)]
        where[longest] = (where[longest] + shift) % array.shape[longest]
        spots.append(tuple(where))
    return array.at[spots[0]].set(low).at[spots[1]].set(largest)


def steps_of(stream_key, shape, cuts, low, largest):
    def one(axis_at, parts):
        heights = jax.random.uniform(jax.random.fold_in(jax.random.fold_in(stream_key, 6), axis_at), (parts,), jnp.float32, low / len(cuts), largest / len(cuts))
        return jnp.repeat(jnp.exp(heights), shape[axis_at] // parts).reshape((-1,) + (1,) * (len(shape) - axis_at - 1))

    loudness = one(*cuts[0])
    for cut in cuts[1:]:
        loudness = loudness * one(*cut)
    return loudness


def bell_draw(own_key, shape, width, reach, shards=(), kind=jnp.bfloat16):
    entries = width * jax.random.normal(own_key, shape, jnp.float32)
    if shards:
        entries = entries * steps_of(own_key, shape, shards, -0.22, 0.18)
    return jnp.clip(entries, -reach, reach).astype(kind)


def setup_inputs(seed: int = 0, part: int = 0) -> dict:
    key_of = jax.random.split(jax.random.key(seed), 7)
    part_splits = jax.random.split(jax.random.fold_in(key_of[6], part), 7)
    return {
        "tokens": bell_draw(part_splits[0], (TOKENS, D), 1.0, 6.0, ((0, 32),)),
        "expert_ids": draw_expert_ids(jax.random.fold_in(jax.random.fold_in(key_of[6], part), 71), part),
        "gate_fixed": with_ends(jax.random.randint(part_splits[2], (TOKENS, TOP), 1, 256), jax.random.fold_in(part_splits[2], 1), 1, 255).astype(jnp.int32),
        "w_gate": bell_draw(key_of[3], (EXPERTS, D, FF), D ** -0.5, 0.125, ((0, 32),)),
        "w_up": bell_draw(key_of[4], (EXPERTS, D, FF), D ** -0.5, 0.125, ((0, 32),)),
        "w_down": bell_draw(key_of[5], (EXPERTS, FF, D), FF ** -0.5, 0.21875, ((0, 32),)),
    }


def route_tables(ids_block, gates_block):
    routes = TOK_DEV * TOP
    slots = EXPERTS * CAP
    flat_ids = ids_block.reshape(routes).astype(jnp.int32)
    one_hot = (flat_ids[:, None] == jnp.arange(EXPERTS, dtype=jnp.int32)[None, :]).astype(jnp.int32)
    before = (jnp.cumsum(one_hot, axis=0) - one_hot).astype(jnp.int32)
    rank_in = jnp.sum(before * one_hot, axis=1).astype(jnp.int32)
    is_kept = rank_in < CAP
    slot_index = (flat_ids * CAP + rank_in).astype(jnp.int32)
    placed = (slot_index[:, None] == jnp.arange(slots, dtype=jnp.int32)[None, :]) & is_kept[:, None]
    dispatch_map = jnp.any(placed.reshape(TOK_DEV, TOP, slots), axis=1).T.astype(jnp.bfloat16)
    weights = gates_block.reshape(routes).astype(jnp.float32) / 256.0
    combine_map = jnp.sum((placed.astype(jnp.float32) * weights[:, None]).reshape(TOK_DEV, TOP, slots), axis=1)
    return dispatch_map, combine_map.astype(jnp.bfloat16)


def expert_ffn(row_block, gate_mat, up_mat, down_mat):
    gate_act = jnp.dot(row_block, gate_mat, preferred_element_type=jnp.float32)
    up_act = jnp.dot(row_block, up_mat, preferred_element_type=jnp.float32)
    hidden = (jax.nn.silu(gate_act) * up_act).astype(jnp.bfloat16)
    return jnp.dot(hidden, down_mat, preferred_element_type=jnp.float32).astype(jnp.bfloat16)


def reference(tokens, expert_ids, gate_fixed, w_gate, w_up, w_down):
    token_blocks = tokens.reshape(DEVS, TOK_DEV, D)
    id_blocks = expert_ids.reshape(DEVS, TOK_DEV, TOP)
    gate_blocks = gate_fixed.reshape(DEVS, TOK_DEV, TOP)

    def build(block):
        dispatch_map, combine_map = route_tables(block[1], block[2])
        outbound = jnp.dot(dispatch_map, block[0], preferred_element_type=jnp.float32).astype(jnp.bfloat16)
        return outbound.reshape(EXPERTS, CAP, D), combine_map

    outbound, combine_maps = lax.map(build, (token_blocks, id_blocks, gate_blocks))
    arrived = jnp.transpose(outbound, (1, 0, 2, 3))

    def serve(item):
        rows = item[0].reshape(DEVS * CAP, D)
        return expert_ffn(rows, item[1], item[2], item[3]).reshape(DEVS, CAP, D)

    expert_out = lax.map(serve, (arrived, w_gate, w_up, w_down))
    results = jnp.transpose(expert_out, (1, 0, 2, 3))

    def combine(item):
        rows = item[0].reshape(EXPERTS * CAP, D)
        return jnp.dot(item[1], rows, preferred_element_type=jnp.float32).astype(jnp.bfloat16)

    mixed = lax.map(combine, (results, combine_maps))
    return mixed.reshape(TOKENS, D)
```

```python
import jax
import jax.numpy as jnp
from jax import lax
from jax.experimental import pallas as pl
from jax.experimental.pallas import tpu as pltpu
from jax.sharding import PartitionSpec as P

SPLIT = (8, 8)


def tables_kernel(split, experts, ids_ref, gates_ref, tokens_ref, *out_refs):
    rows_refs, maps_refs = out_refs[: len(split)], out_refs[len(split) :]
    tok_dev, top_count = ids_ref.shape
    ids, gates = ids_ref[...], gates_ref[...]
    expert = lax.broadcasted_iota(jnp.int32, (tok_dev, experts), 1)
    named = jnp.zeros((tok_dev, experts), jnp.float32)
    weight = jnp.zeros((tok_dev, experts), jnp.float32)
    for k in range(top_count):
        hit = ids[:, k : k + 1] == expert
        named = jnp.where(hit, 1.0, named)
        weight = jnp.where(hit, gates[:, k : k + 1].astype(jnp.float32), weight)
    earlier = lax.broadcasted_iota(jnp.int32, (tok_dev, tok_dev), 1) < lax.broadcasted_iota(
        jnp.int32, (tok_dev, tok_dev), 0
    )
    rank = jnp.dot(
        jnp.where(earlier, 1.0, 0.0).astype(jnp.bfloat16),
        named.astype(jnp.bfloat16),
        preferred_element_type=jnp.float32,
    )
    rank = jnp.where(named > 0.0, rank, -1.0).astype(jnp.bfloat16)
    weight = weight.astype(jnp.bfloat16)
    tokens = tokens_ref[...]
    first = 0
    for size, rows_ref, map_ref in zip(split, rows_refs, maps_refs):
        slots = experts * size
        row = lax.broadcasted_iota(jnp.int32, (experts, slots), 1)
        spread = jnp.where(
            row // size == lax.broadcasted_iota(jnp.int32, (experts, slots), 0), 1.0, 0.0
        ).astype(jnp.bfloat16)
        slot = lax.broadcasted_iota(jnp.int32, (tok_dev, slots), 1) % size + first
        placed = jnp.dot(rank, spread, preferred_element_type=jnp.float32) == slot.astype(
            jnp.float32
        )
        share = jnp.dot(weight, spread, preferred_element_type=jnp.float32) * (1.0 / 256.0)
        map_ref[...] = jnp.where(placed, share, 0.0).astype(map_ref.dtype)
        rows_ref[...] = lax.dot_general(
            jnp.where(placed, 1.0, 0.0).astype(jnp.bfloat16),
            tokens,
            (((0,), (0,)), ((), ())),
            preferred_element_type=jnp.float32,
        ).astype(rows_ref.dtype)
        first += size


def build_tables(ids, gates, tokens, experts, split):
    tok_dev, width = tokens.shape
    shapes = [jax.ShapeDtypeStruct((experts * s, width), jnp.bfloat16) for s in split] + [
        jax.ShapeDtypeStruct((tok_dev, experts * s), jnp.bfloat16) for s in split
    ]
    whole = pl.BlockSpec(memory_space=pltpu.VMEM)
    outs = pl.pallas_call(
        lambda *refs: tables_kernel(split, experts, *refs),
        out_shape=shapes,
        in_specs=[whole] * 3,
        out_specs=[whole] * len(shapes),
        compiler_params=pltpu.CompilerParams(vmem_limit_bytes=24 * 1024 * 1024),
        name="tables",
    )(ids, gates, tokens)
    return outs[: len(split)], outs[len(split) :]


def expert_ffn(arrived, gate_mat, up_mat, down_mat):
    width = arrived.shape[-1]
    row_block = arrived.reshape(-1, width)
    gate_act = jnp.dot(row_block, gate_mat, preferred_element_type=jnp.float32)
    up_act = jnp.dot(row_block, up_mat, preferred_element_type=jnp.float32)
    hidden = (jax.nn.silu(gate_act) * up_act).astype(jnp.bfloat16)
    output = jnp.dot(hidden, down_mat, preferred_element_type=jnp.float32).astype(jnp.bfloat16)
    return output.reshape(arrived.shape)


def on_device(tokens, expert_ids, gate_fixed, w_gate, w_up, w_down):
    width = tokens.shape[1]
    experts = lax.axis_size(("node", "chip")) * w_gate.shape[0]
    outbound, maps = build_tables(expert_ids, gate_fixed, tokens, experts, SPLIT)

    def exchange(block):
        return lax.all_to_all(block, ("node", "chip"), split_axis=0, concat_axis=0, tiled=True)

    arrived = [exchange(rows.reshape(experts, -1, width)) for rows in outbound]
    served = [expert_ffn(block, w_gate[0], w_up[0], w_down[0]) for block in arrived]
    results = [exchange(block) for block in served]
    total = 0.0
    for combine_map, result in zip(maps, results):
        total = total + jnp.dot(
            combine_map, result.reshape(-1, width), preferred_element_type=jnp.float32
        )
    return total.astype(jnp.bfloat16)


def solution(mesh):
    return jax.shard_map(
        on_device,
        mesh=mesh,
        in_specs=(
            P(("dp", "node", "chip"), None),
            P(("dp", "node", "chip"), None),
            P(("dp", "node", "chip"), None),
            P(("node", "chip"), None, None),
            P(("node", "chip"), None, None),
            P(("node", "chip"), None, None),
        ),
        out_specs=P(("dp", "node", "chip"), None),
        check_vma=False,
    )
```

```python
import jax
import jax.numpy as jnp
from jax import lax
from jax.experimental import pallas as pl
from jax.experimental.pallas import tpu as pltpu
from jax.sharding import PartitionSpec as P

MIB = 1024 * 1024


def tables_kernel(experts, ids_ref, gates_ref, tokens_ref, rows_ref, map_ref, tokens, arrived):
    fetch = pltpu.make_async_copy(tokens_ref, tokens, arrived)
    fetch.start()
    top_count, tok_dev = ids_ref.shape
    slots = rows_ref.shape[0]
    capacity = slots // experts
    ids, gates = ids_ref[...], gates_ref[...].astype(jnp.float32)
    expert = lax.broadcasted_iota(jnp.int32, (experts, tok_dev), 0)
    named = jnp.zeros((experts, tok_dev), jnp.float32)
    weight = jnp.zeros((experts, tok_dev), jnp.float32)
    for k in range(top_count):
        hit = ids[k : k + 1, :] == expert
        named = jnp.where(hit, 1.0, named)
        weight = jnp.where(hit, gates[k : k + 1, :], weight)
    earlier = lax.broadcasted_iota(jnp.int32, (tok_dev, tok_dev), 0) < lax.broadcasted_iota(
        jnp.int32, (tok_dev, tok_dev), 1
    )
    rank = jnp.dot(
        named.astype(jnp.bfloat16),
        jnp.where(earlier, 1.0, 0.0).astype(jnp.bfloat16),
        preferred_element_type=jnp.float32,
    )
    rank = jnp.where(named > 0.0, rank, -1.0).astype(jnp.bfloat16)
    row = lax.broadcasted_iota(jnp.int32, (slots, experts), 0)
    spread = jnp.where(
        row // capacity == lax.broadcasted_iota(jnp.int32, (slots, experts), 1), 1.0, 0.0
    ).astype(jnp.bfloat16)
    slot = lax.broadcasted_iota(jnp.int32, (slots, tok_dev), 0) % capacity
    placed = jnp.dot(spread, rank, preferred_element_type=jnp.float32) == slot.astype(
        jnp.float32
    )
    share = jnp.dot(spread, weight.astype(jnp.bfloat16), preferred_element_type=jnp.float32)
    map_ref[...] = jnp.where(placed, share * (1.0 / 256.0), 0.0).astype(map_ref.dtype)
    chosen = jnp.where(placed, 1.0, 0.0).astype(jnp.bfloat16)
    fetch.wait()
    rows_ref[...] = jnp.dot(chosen, tokens[...], preferred_element_type=jnp.float32).astype(
        rows_ref.dtype
    )


def build_tables(ids, gates, tokens, experts, capacity):
    tok_dev, width = tokens.shape
    whole = pl.BlockSpec(memory_space=pltpu.VMEM)
    return pl.pallas_call(
        lambda *refs: tables_kernel(experts, *refs),
        out_shape=(
            jax.ShapeDtypeStruct((experts * capacity, width), jnp.bfloat16),
            jax.ShapeDtypeStruct((experts * capacity, tok_dev), jnp.bfloat16),
        ),
        in_specs=[whole, whole, pl.BlockSpec(memory_space=pl.ANY)],
        out_specs=(whole, whole),
        scratch_shapes=[
            pltpu.VMEM((tok_dev, width), jnp.bfloat16),
            pltpu.SemaphoreType.DMA,
        ],
        compiler_params=pltpu.CompilerParams(vmem_limit_bytes=24 * MIB),
        name="tables",
    )(ids.T, gates.T, tokens)


def ffn_kernel(step, rows_ref, gate_ref, up_ref, down_ref, out_ref, up, down, gated, hidden, arrived):
    fetch_up = pltpu.make_async_copy(up_ref, up, arrived.at[0])
    fetch_down = pltpu.make_async_copy(down_ref, down, arrived.at[1])
    fetch_up.start()
    fetch_down.start()
    rows = rows_ref[...]
    for at in range(0, gate_ref.shape[1], step):
        part = pl.ds(at, step)
        gate_act = jnp.dot(rows, gate_ref[:, part], preferred_element_type=jnp.float32)
        gated[:, part] = gate_act / (1.0 + jnp.exp(-gate_act))
    fetch_up.wait()
    for at in range(0, gate_ref.shape[1], step):
        part = pl.ds(at, step)
        up_act = jnp.dot(rows, up[:, part], preferred_element_type=jnp.float32)
        hidden[:, part] = (gated[:, part] * up_act).astype(hidden.dtype)
    fetch_down.wait()
    for at in range(0, down.shape[1], step):
        part = pl.ds(at, step)
        out_ref[:, part] = jnp.dot(
            hidden[...], down[:, part], preferred_element_type=jnp.float32
        ).astype(out_ref.dtype)


def expert_ffn(rows, gate_mat, up_mat, down_mat):
    count, width = rows.shape
    ff = gate_mat.shape[1]
    whole = pl.BlockSpec(memory_space=pltpu.VMEM)
    away = pl.BlockSpec(memory_space=pl.ANY)
    return pl.pallas_call(
        lambda *refs: ffn_kernel(256, *refs),
        out_shape=jax.ShapeDtypeStruct((count, width), jnp.bfloat16),
        in_specs=[whole, whole, away, away],
        out_specs=whole,
        scratch_shapes=[
            pltpu.VMEM((width, ff), jnp.bfloat16),
            pltpu.VMEM((ff, width), jnp.bfloat16),
            pltpu.VMEM((count, ff), jnp.float32),
            pltpu.VMEM((count, ff), jnp.bfloat16),
            pltpu.SemaphoreType.DMA((2,)),
        ],
        compiler_params=pltpu.CompilerParams(vmem_limit_bytes=32 * MIB),
        cost_estimate=pl.CostEstimate(
            flops=6 * count * width * ff,
            bytes_accessed=6 * width * ff + 4 * count * width,
            transcendentals=count * ff,
        ),
        name="ffn",
    )(rows, gate_mat, up_mat, down_mat)


def combine_kernel(map_ref, results_ref, out_ref):
    out_ref[...] = lax.dot_general(
        map_ref[...],
        results_ref[...],
        (((0,), (0,)), ((), ())),
        preferred_element_type=jnp.float32,
    ).astype(out_ref.dtype)


def combine(combine_map, results, step=512):
    slots, width = results.shape
    tok_dev = combine_map.shape[1]
    return pl.pallas_call(
        combine_kernel,
        out_shape=jax.ShapeDtypeStruct((tok_dev, width), jnp.bfloat16),
        grid=(width // step,),
        in_specs=[
            pl.BlockSpec((slots, tok_dev), lambda i: (0, 0)),
            pl.BlockSpec((slots, step), lambda i: (0, i)),
        ],
        out_specs=pl.BlockSpec((tok_dev, step), lambda i: (0, i)),
        compiler_params=pltpu.CompilerParams(vmem_limit_bytes=16 * MIB),
        name="combine",
    )(combine_map, results)


def on_device(tokens, expert_ids, gate_fixed, w_gate, w_up, w_down):
    tok_dev, width = tokens.shape
    top_count = expert_ids.shape[1]
    experts = lax.axis_size(("node", "chip")) * w_gate.shape[0]
    capacity = tok_dev * top_count // experts
    outbound, combine_map = build_tables(expert_ids, gate_fixed, tokens, experts, capacity)

    def exchange(rows):
        blocks = rows.reshape(experts, capacity, width)
        return lax.all_to_all(
            blocks, ("node", "chip"), split_axis=0, concat_axis=0, tiled=True
        ).reshape(experts * capacity, width)

    served = expert_ffn(exchange(outbound), w_gate[0], w_up[0], w_down[0])
    return combine(combine_map, exchange(served))


def solution(mesh):
    return jax.shard_map(
        on_device,
        mesh=mesh,
        in_specs=(
            P(("dp", "node", "chip"), None),
            P(("dp", "node", "chip"), None),
            P(("dp", "node", "chip"), None),
            P(("node", "chip"), None, None),
            P(("node", "chip"), None, None),
            P(("node", "chip"), None, None),
        ),
        out_specs=P(("dp", "node", "chip"), None),
        check_vma=False,
    )
```

```python
import jax
import jax.numpy as jnp
from jax import lax
from jax.experimental import pallas as pl
from jax.experimental.pallas import tpu as pltpu
from jax.sharding import PartitionSpec as P

MIB = 1024 * 1024


def tables_kernel(
    experts,
    ids_ref,
    gates_ref,
    tokens_ref,
    rows_ref,
    map_ref,
    ids_here,
    gates_here,
    tokens,
    rows,
    arrived,
    left,
):
    fetch_ids = pltpu.make_async_copy(ids_ref, ids_here, arrived.at[0])
    fetch_gates = pltpu.make_async_copy(gates_ref, gates_here, arrived.at[1])
    fetch_tokens = pltpu.make_async_copy(tokens_ref, tokens, arrived.at[2])
    fetch_ids.start()
    fetch_gates.start()
    fetch_tokens.start()
    top_count, tok_dev = ids_ref.shape
    slots = rows_ref.shape[0]
    capacity = slots // experts
    fetch_ids.wait()
    fetch_gates.wait()
    ids, gates = ids_here[...], gates_here[...].astype(jnp.float32)
    expert = lax.broadcasted_iota(jnp.int32, (experts, tok_dev), 0)
    named = jnp.zeros((experts, tok_dev), jnp.float32)
    weight = jnp.zeros((experts, tok_dev), jnp.float32)
    for k in range(top_count):
        hit = ids[k : k + 1, :] == expert
        named = jnp.where(hit, 1.0, named)
        weight = jnp.where(hit, gates[k : k + 1, :], weight)
    earlier = lax.broadcasted_iota(jnp.int32, (tok_dev, tok_dev), 0) < lax.broadcasted_iota(
        jnp.int32, (tok_dev, tok_dev), 1
    )
    rank = jnp.dot(
        named.astype(jnp.bfloat16),
        jnp.where(earlier, 1.0, 0.0).astype(jnp.bfloat16),
        preferred_element_type=jnp.float32,
    )
    rank = jnp.where(named > 0.0, rank, -1.0).astype(jnp.bfloat16)
    row = lax.broadcasted_iota(jnp.int32, (slots, experts), 0)
    spread = jnp.where(
        row // capacity == lax.broadcasted_iota(jnp.int32, (slots, experts), 1), 1.0, 0.0
    ).astype(jnp.bfloat16)
    slot = lax.broadcasted_iota(jnp.int32, (slots, tok_dev), 0) % capacity
    placed = jnp.dot(spread, rank, preferred_element_type=jnp.float32) == slot.astype(
        jnp.float32
    )
    share = jnp.dot(spread, weight.astype(jnp.bfloat16), preferred_element_type=jnp.float32)
    map_ref[...] = jnp.where(placed, share * (1.0 / 256.0), 0.0).astype(map_ref.dtype)
    chosen = jnp.where(placed, 1.0, 0.0).astype(jnp.bfloat16)
    fetch_tokens.wait()
    step = rows.shape[1] // left.shape[0]
    stores = []
    for i in range(left.shape[0]):
        part = pl.ds(i * step, step)
        rows[:, part] = jnp.dot(
            chosen, tokens[:, part], preferred_element_type=jnp.float32
        ).astype(rows.dtype)
        stores.append(pltpu.make_async_copy(rows.at[:, part], rows_ref.at[:, part], left.at[i]))
        stores[-1].start()
    for store in stores:
        store.wait()


def build_tables(ids, gates, tokens, experts, capacity):
    tok_dev, width = tokens.shape
    whole = pl.BlockSpec(memory_space=pltpu.VMEM)
    return pl.pallas_call(
        lambda *refs: tables_kernel(experts, *refs),
        out_shape=(
            jax.ShapeDtypeStruct((experts * capacity, width), jnp.bfloat16),
            jax.ShapeDtypeStruct((experts * capacity, tok_dev), jnp.bfloat16),
        ),
        in_specs=[pl.BlockSpec(memory_space=pltpu.HBM)] * 3,
        out_specs=(pl.BlockSpec(memory_space=pltpu.HBM), whole),
        scratch_shapes=[
            pltpu.VMEM(ids.T.shape, jnp.int32),
            pltpu.VMEM(gates.T.shape, jnp.int32),
            pltpu.VMEM((tok_dev, width), jnp.bfloat16),
            pltpu.VMEM((experts * capacity, width), jnp.bfloat16),
            pltpu.SemaphoreType.DMA((3,)),
            pltpu.SemaphoreType.DMA((4,)),
        ],
        compiler_params=pltpu.CompilerParams(vmem_limit_bytes=56 * MIB),
        name="tables",
    )(ids.T, gates.T, tokens)


def ffn_kernel(step, rows_ref, gate_ref, up_ref, down_ref, out_ref, up, down, gated, hidden, arrived):
    fetch_up = pltpu.make_async_copy(up_ref, up, arrived.at[0])
    fetch_down = pltpu.make_async_copy(down_ref, down, arrived.at[1])
    fetch_up.start()
    fetch_down.start()

    def tiles(columns):
        for at in range(0, columns, step):
            for top in range(0, rows_ref.shape[0], step):
                yield pl.ds(top, step), pl.ds(at, step)

    def product(left, right):
        return jnp.dot(left, right, preferred_element_type=jnp.float32)

    for part, cols in tiles(gate_ref.shape[1]):
        gate_act = product(rows_ref[part, :], gate_ref[:, cols])
        gated[part, cols] = gate_act / (1.0 + jnp.exp(-gate_act))
    fetch_up.wait()
    for part, cols in tiles(gate_ref.shape[1]):
        up_act = product(rows_ref[part, :], up[:, cols])
        hidden[part, cols] = (gated[part, cols] * up_act).astype(hidden.dtype)
    fetch_down.wait()
    for part, cols in tiles(out_ref.shape[1]):
        out_ref[part, cols] = product(hidden[part, :], down[:, cols]).astype(out_ref.dtype)


def expert_ffn(rows, gate_mat, up_mat, down_mat):
    count, width = rows.shape
    ff = gate_mat.shape[1]
    whole = pl.BlockSpec(memory_space=pltpu.VMEM)
    away = pl.BlockSpec(memory_space=pltpu.HBM)
    return pl.pallas_call(
        lambda *refs: ffn_kernel(256, *refs),
        out_shape=jax.ShapeDtypeStruct((count, width), jnp.bfloat16),
        in_specs=[whole, whole, away, away],
        out_specs=whole,
        scratch_shapes=[
            pltpu.VMEM((width, ff), jnp.bfloat16),
            pltpu.VMEM((ff, width), jnp.bfloat16),
            pltpu.VMEM((count, ff), jnp.float32),
            pltpu.VMEM((count, ff), jnp.bfloat16),
            pltpu.SemaphoreType.DMA((2,)),
        ],
        compiler_params=pltpu.CompilerParams(vmem_limit_bytes=44 * MIB),
        cost_estimate=pl.CostEstimate(
            flops=6 * count * width * ff,
            bytes_accessed=6 * width * ff + 4 * count * width,
            transcendentals=count * ff,
        ),
        name="ffn",
    )(rows, gate_mat, up_mat, down_mat)


def combine_kernel(map_ref, results_ref, out_ref):
    out_ref[...] = lax.dot_general(
        map_ref[...],
        results_ref[...],
        (((0,), (0,)), ((), ())),
        preferred_element_type=jnp.float32,
    ).astype(out_ref.dtype)


def combine(combine_map, results):
    whole = pl.BlockSpec(memory_space=pltpu.VMEM)
    return pl.pallas_call(
        combine_kernel,
        out_shape=jax.ShapeDtypeStruct((combine_map.shape[1], results.shape[1]), jnp.bfloat16),
        in_specs=[whole] * 2,
        out_specs=whole,
        compiler_params=pltpu.CompilerParams(vmem_limit_bytes=16 * MIB),
        name="combine",
    )(combine_map, results)


def on_device(tokens, expert_ids, gate_fixed, w_gate, w_up, w_down):
    tok_dev, width = tokens.shape
    top_count = expert_ids.shape[1]
    experts = lax.axis_size(("node", "chip")) * w_gate.shape[0]
    capacity = tok_dev * top_count // experts
    outbound, combine_map = build_tables(expert_ids, gate_fixed, tokens, experts, capacity)

    def exchange(rows):
        blocks = rows.reshape(experts, capacity, width)
        return lax.all_to_all(
            blocks, ("node", "chip"), split_axis=0, concat_axis=0, tiled=True
        ).reshape(experts * capacity, width)

    served = expert_ffn(exchange(outbound), w_gate[0], w_up[0], w_down[0])
    return combine(combine_map, exchange(served))


def solution(mesh):
    return jax.shard_map(
        on_device,
        mesh=mesh,
        in_specs=(
            P(("dp", "node", "chip"), None),
            P(("dp", "node", "chip"), None),
            P(("dp", "node", "chip"), None),
            P(("node", "chip"), None, None),
            P(("node", "chip"), None, None),
            P(("node", "chip"), None, None),
        ),
        out_specs=P(("dp", "node", "chip"), None),
        check_vma=False,
    )
```

```python
import jax
import jax.numpy as jnp
from jax import lax
from jax.experimental import pallas as pl
from jax.experimental.pallas import tpu as pltpu
from jax.sharding import PartitionSpec as P

MIB = 1024 * 1024
TILE = 256
PIECES = (((2048,), (2048,)), ((256, 256, 1536), (2048,)))


def tables_kernel(experts, pieces, ids_ref, gates_ref, tokens_ref, *refs):
    rows_refs, map_ref = refs[: len(pieces)], refs[len(pieces)]
    ids_here, gates_here, tokens, rows, combine_map, arrived, left = refs[len(pieces) + 1 :]
    fetch_ids = pltpu.make_async_copy(ids_ref, ids_here, arrived.at[0])
    fetch_gates = pltpu.make_async_copy(gates_ref, gates_here, arrived.at[1])
    fetch_tokens = pltpu.make_async_copy(tokens_ref, tokens, arrived.at[2])
    fetch_ids.start()
    fetch_gates.start()
    fetch_tokens.start()
    top_count, tok_dev = ids_ref.shape
    slots = rows.shape[0]
    capacity = slots // experts
    row = lax.broadcasted_iota(jnp.int32, (slots, experts), 0)
    spread = jnp.where(
        row // capacity == lax.broadcasted_iota(jnp.int32, (slots, experts), 1), 1.0, 0.0
    ).astype(jnp.bfloat16)
    slot = lax.broadcasted_iota(jnp.int32, (slots, tok_dev), 0) % capacity
    earlier = lax.broadcasted_iota(jnp.int32, (tok_dev, tok_dev), 0) < lax.broadcasted_iota(
        jnp.int32, (tok_dev, tok_dev), 1
    )
    expert = lax.broadcasted_iota(jnp.int32, (experts, tok_dev), 0)
    fetch_ids.wait()
    ids = ids_here[...]
    named = jnp.zeros((experts, tok_dev), jnp.float32)
    for k in range(top_count):
        named = jnp.where(ids[k : k + 1, :] == expert, 1.0, named)
    rank = jnp.dot(
        named.astype(jnp.bfloat16),
        jnp.where(earlier, 1.0, 0.0).astype(jnp.bfloat16),
        preferred_element_type=jnp.float32,
    )
    rank = jnp.where(named > 0.0, rank, -1.0).astype(jnp.bfloat16)
    placed = jnp.dot(spread, rank, preferred_element_type=jnp.float32) == slot.astype(
        jnp.float32
    )
    chosen = jnp.where(placed, 1.0, 0.0).astype(jnp.bfloat16)
    fetch_tokens.wait()
    stores = []
    first = 0
    for width, rows_ref in zip(pieces, rows_refs):
        for at in range(0, width, TILE):
            part = pl.ds(first + at, TILE)
            rows[:, part] = jnp.dot(
                chosen, tokens[:, part], preferred_element_type=jnp.float32
            ).astype(rows.dtype)
            stores.append(
                pltpu.make_async_copy(
                    rows.at[:, part], rows_ref.at[:, pl.ds(at, TILE)], left.at[len(stores)]
                )
            )
            stores[-1].start()
        first += width
    fetch_gates.wait()
    gates = gates_here[...].astype(jnp.float32)
    weight = jnp.zeros((experts, tok_dev), jnp.float32)
    for k in range(top_count):
        weight = jnp.where(ids[k : k + 1, :] == expert, gates[k : k + 1, :], weight)
    share = jnp.dot(spread, weight.astype(jnp.bfloat16), preferred_element_type=jnp.float32)
    combine_map[...] = jnp.where(placed, share * (1.0 / 256.0), 0.0).astype(combine_map.dtype)
    stores.append(pltpu.make_async_copy(combine_map, map_ref, left.at[len(stores)]))
    stores[-1].start()
    for store in stores:
        store.wait()


def build_tables(ids, gates, tokens, experts, capacity, pieces):
    tok_dev, width = tokens.shape
    slots = experts * capacity
    away = pl.BlockSpec(memory_space=pltpu.HBM)
    outs = pl.pallas_call(
        lambda *refs: tables_kernel(experts, pieces, *refs),
        out_shape=[jax.ShapeDtypeStruct((slots, piece), jnp.bfloat16) for piece in pieces]
        + [jax.ShapeDtypeStruct((slots, tok_dev), jnp.bfloat16)],
        in_specs=[away] * 3,
        out_specs=[away] * (len(pieces) + 1),
        scratch_shapes=[
            pltpu.VMEM(ids.T.shape, jnp.int32),
            pltpu.VMEM(gates.T.shape, jnp.int32),
            pltpu.VMEM((tok_dev, width), jnp.bfloat16),
            pltpu.VMEM((slots, width), jnp.bfloat16),
            pltpu.VMEM((slots, tok_dev), jnp.bfloat16),
            pltpu.SemaphoreType.DMA((3,)),
            pltpu.SemaphoreType.DMA((width // TILE + 1,)),
        ],
        compiler_params=pltpu.CompilerParams(vmem_limit_bytes=56 * MIB),
        name=f"tables_{len(pieces)}",
    )(ids.T, gates.T, tokens)
    return outs[:-1], outs[-1]


def ffn_kernel(step, count, *refs):
    rows_refs, (gate_ref, up_ref, down_ref), out_refs = refs[:count], refs[count : count + 3], refs[count + 3 : -5]
    up, down, gated, hidden, arrived = refs[-5:]
    fetch_up = pltpu.make_async_copy(up_ref, up, arrived.at[0])
    fetch_down = pltpu.make_async_copy(down_ref, down, arrived.at[1])
    fetch_up.start()
    fetch_down.start()

    def tiles(columns):
        for at in range(0, columns, step):
            for top in range(0, hidden.shape[0], step):
                yield pl.ds(top, step), pl.ds(at, step)

    def product(left, right):
        return jnp.dot(left, right, preferred_element_type=jnp.float32)

    def from_rows(part, weight_ref, cols):
        total, first = None, 0
        for rows_ref in rows_refs:
            depth = rows_ref.shape[1]
            term = product(rows_ref[part, :], weight_ref[pl.ds(first, depth), cols])
            total = term if total is None else total + term
            first += depth
        return total

    for part, cols in tiles(gate_ref.shape[1]):
        gate_act = from_rows(part, gate_ref, cols)
        gated[part, cols] = gate_act / (1.0 + jnp.exp(-gate_act))
    fetch_up.wait()
    for part, cols in tiles(gate_ref.shape[1]):
        up_act = from_rows(part, up, cols)
        hidden[part, cols] = (gated[part, cols] * up_act).astype(hidden.dtype)
    fetch_down.wait()
    first = 0
    for out_ref in out_refs:
        for part, cols in tiles(out_ref.shape[1]):
            weights = down[:, pl.ds(first + cols.start, step)]
            out_ref[part, cols] = product(hidden[part, :], weights).astype(out_ref.dtype)
        first += out_ref.shape[1]


def expert_ffn(rows, gate_mat, up_mat, down_mat, pieces):
    count = rows[0].shape[0]
    width, ff = gate_mat.shape
    whole = pl.BlockSpec(memory_space=pltpu.VMEM)
    away = pl.BlockSpec(memory_space=pltpu.HBM)
    return pl.pallas_call(
        lambda *refs: ffn_kernel(256, len(rows), *refs),
        out_shape=[jax.ShapeDtypeStruct((count, piece), jnp.bfloat16) for piece in pieces],
        in_specs=[whole] * (len(rows) + 1) + [away, away],
        out_specs=[whole] * len(pieces),
        scratch_shapes=[
            pltpu.VMEM((width, ff), jnp.bfloat16),
            pltpu.VMEM((ff, width), jnp.bfloat16),
            pltpu.VMEM((count, ff), jnp.float32),
            pltpu.VMEM((count, ff), jnp.bfloat16),
            pltpu.SemaphoreType.DMA((2,)),
        ],
        compiler_params=pltpu.CompilerParams(vmem_limit_bytes=44 * MIB),
        cost_estimate=pl.CostEstimate(
            flops=6 * count * width * ff,
            bytes_accessed=6 * width * ff + 4 * count * width,
            transcendentals=count * ff,
        ),
        name=f"ffn_{len(rows)}_{len(pieces)}",
    )(*rows, gate_mat, up_mat, down_mat)


def combine_kernel(map_ref, *refs):
    results_refs, out_ref = refs[:-1], refs[-1]
    first = 0
    for results_ref in results_refs:
        width = results_ref.shape[1]
        out_ref[:, pl.ds(first, width)] = lax.dot_general(
            map_ref[...],
            results_ref[...],
            (((0,), (0,)), ((), ())),
            preferred_element_type=jnp.float32,
        ).astype(out_ref.dtype)
        first += width


def combine(combine_map, results):
    whole = pl.BlockSpec(memory_space=pltpu.VMEM)
    width = sum(result.shape[1] for result in results)
    return pl.pallas_call(
        combine_kernel,
        out_shape=jax.ShapeDtypeStruct((combine_map.shape[1], width), jnp.bfloat16),
        in_specs=[whole] * (len(results) + 1),
        out_specs=whole,
        compiler_params=pltpu.CompilerParams(vmem_limit_bytes=16 * MIB),
        name=f"combine_{len(results)}",
    )(combine_map, *results)


def layer(out_pieces, back_pieces, tokens, expert_ids, gate_fixed, w_gate, w_up, w_down):
    tok_dev, width = tokens.shape
    top_count = expert_ids.shape[1]
    experts = lax.axis_size(("node", "chip")) * w_gate.shape[0]
    capacity = tok_dev * top_count // experts
    outbound, combine_map = build_tables(
        expert_ids, gate_fixed, tokens, experts, capacity, out_pieces
    )

    def exchange(rows):
        blocks = rows.reshape(experts, capacity, rows.shape[1])
        return lax.all_to_all(
            blocks, ("node", "chip"), split_axis=0, concat_axis=0, tiled=True
        ).reshape(rows.shape)

    arrived = [exchange(rows) for rows in outbound]
    served = expert_ffn(arrived, w_gate[0], w_up[0], w_down[0], back_pieces)
    return combine(combine_map, [exchange(rows) for rows in served])


def on_device(*args):
    return lax.cond(
        lax.axis_index("dp") % 2 == 0,
        lambda *a: layer(*PIECES[0], *a),
        lambda *a: layer(*PIECES[1], *a),
        *args,
    )


def solution(mesh):
    return jax.shard_map(
        on_device,
        mesh=mesh,
        in_specs=(
            P(("dp", "node", "chip"), None),
            P(("dp", "node", "chip"), None),
            P(("dp", "node", "chip"), None),
            P(("node", "chip"), None, None),
            P(("node", "chip"), None, None),
            P(("node", "chip"), None, None),
        ),
        out_specs=P(("dp", "node", "chip"), None),
        check_vma=False,
    )
```

```python
import jax
import jax.numpy as jnp
from jax import lax
from jax.experimental import pallas as pl
from jax.experimental.pallas import tpu as pltpu
from jax.sharding import PartitionSpec as P

MIB = 1024 * 1024
TILE = 128
PIECES = (((2048,), (2048,)), ((128, 128, 1792), (2048,)))


def tables_kernel(experts, pieces, ids_ref, gates_ref, tokens_ref, *refs):
    rows_refs, map_ref = refs[: len(pieces)], refs[len(pieces)]
    ids_here, gates_here, tokens, rows, combine_map, arrived, left = refs[len(pieces) + 1 :]
    fetch_ids = pltpu.make_async_copy(ids_ref, ids_here, arrived.at[0])
    fetch_gates = pltpu.make_async_copy(gates_ref, gates_here, arrived.at[1])
    fetch_tokens = pltpu.make_async_copy(tokens_ref, tokens, arrived.at[2])
    fetch_ids.start()
    fetch_gates.start()
    fetch_tokens.start()
    top_count, tok_dev = ids_ref.shape
    slots = rows.shape[0]
    capacity = slots // experts
    row = lax.broadcasted_iota(jnp.int32, (slots, experts), 0)
    spread = jnp.where(
        row // capacity == lax.broadcasted_iota(jnp.int32, (slots, experts), 1), 1.0, 0.0
    ).astype(jnp.bfloat16)
    slot = lax.broadcasted_iota(jnp.int32, (slots, tok_dev), 0) % capacity
    earlier = lax.broadcasted_iota(jnp.int32, (tok_dev, tok_dev), 0) < lax.broadcasted_iota(
        jnp.int32, (tok_dev, tok_dev), 1
    )
    expert = lax.broadcasted_iota(jnp.int32, (experts, tok_dev), 0)
    fetch_ids.wait()
    ids = ids_here[...]
    named = jnp.zeros((experts, tok_dev), jnp.float32)
    for k in range(top_count):
        named = jnp.where(ids[k : k + 1, :] == expert, 1.0, named)
    rank = jnp.dot(
        named.astype(jnp.bfloat16),
        jnp.where(earlier, 1.0, 0.0).astype(jnp.bfloat16),
        preferred_element_type=jnp.float32,
    )
    rank = jnp.where(named > 0.0, rank, -1.0).astype(jnp.bfloat16)
    placed = jnp.dot(spread, rank, preferred_element_type=jnp.float32) == slot.astype(
        jnp.float32
    )
    chosen = jnp.where(placed, 1.0, 0.0).astype(jnp.bfloat16)
    fetch_tokens.wait()
    stores = []
    first = 0
    for width, rows_ref in zip(pieces, rows_refs):
        for at in range(0, width, TILE):
            part = pl.ds(first + at, TILE)
            rows[:, part] = jnp.dot(
                chosen, tokens[:, part], preferred_element_type=jnp.float32
            ).astype(rows.dtype)
            stores.append(
                pltpu.make_async_copy(
                    rows.at[:, part], rows_ref.at[:, pl.ds(at, TILE)], left.at[len(stores)]
                )
            )
            stores[-1].start()
        first += width
    fetch_gates.wait()
    gates = gates_here[...].astype(jnp.float32)
    weight = jnp.zeros((experts, tok_dev), jnp.float32)
    for k in range(top_count):
        weight = jnp.where(ids[k : k + 1, :] == expert, gates[k : k + 1, :], weight)
    share = jnp.dot(spread, weight.astype(jnp.bfloat16), preferred_element_type=jnp.float32)
    combine_map[...] = jnp.where(placed, share * (1.0 / 256.0), 0.0).astype(combine_map.dtype)
    stores.append(pltpu.make_async_copy(combine_map, map_ref, left.at[len(stores)]))
    stores[-1].start()
    for store in stores:
        store.wait()


def build_tables(ids, gates, tokens, experts, capacity, pieces):
    tok_dev, width = tokens.shape
    slots = experts * capacity
    away = pl.BlockSpec(memory_space=pltpu.HBM)
    outs = pl.pallas_call(
        lambda *refs: tables_kernel(experts, pieces, *refs),
        out_shape=[jax.ShapeDtypeStruct((slots, piece), jnp.bfloat16) for piece in pieces]
        + [jax.ShapeDtypeStruct((slots, tok_dev), jnp.bfloat16)],
        in_specs=[away] * 3,
        out_specs=[away] * (len(pieces) + 1),
        scratch_shapes=[
            pltpu.VMEM(ids.T.shape, jnp.int32),
            pltpu.VMEM(gates.T.shape, jnp.int32),
            pltpu.VMEM((tok_dev, width), jnp.bfloat16),
            pltpu.VMEM((slots, width), jnp.bfloat16),
            pltpu.VMEM((slots, tok_dev), jnp.bfloat16),
            pltpu.SemaphoreType.DMA((3,)),
            pltpu.SemaphoreType.DMA((width // TILE + 1,)),
        ],
        compiler_params=pltpu.CompilerParams(vmem_limit_bytes=56 * MIB),
        name=f"tables_{len(pieces)}",
    )(ids.T, gates.T, tokens)
    return outs[:-1], outs[-1]


def ffn_kernel(step, count, *refs):
    rows_refs, (gate_ref, up_ref, down_ref), out_refs = refs[:count], refs[count : count + 3], refs[count + 3 : -5]
    up, down, gated, hidden, arrived = refs[-5:]
    fetch_up = pltpu.make_async_copy(up_ref, up, arrived.at[0])
    fetch_down = pltpu.make_async_copy(down_ref, down, arrived.at[1])
    fetch_up.start()
    fetch_down.start()

    def tiles(columns):
        for at in range(0, columns, step):
            for top in range(0, hidden.shape[0], step):
                yield pl.ds(top, step), pl.ds(at, step)

    def product(left, right):
        return jnp.dot(left, right, preferred_element_type=jnp.float32)

    def from_rows(part, weight_ref, cols):
        total, first = None, 0
        for rows_ref in rows_refs:
            depth = rows_ref.shape[1]
            term = product(rows_ref[part, :], weight_ref[pl.ds(first, depth), cols])
            total = term if total is None else total + term
            first += depth
        return total

    for part, cols in tiles(gate_ref.shape[1]):
        gate_act = from_rows(part, gate_ref, cols)
        gated[part, cols] = gate_act / (1.0 + jnp.exp(-gate_act))
    fetch_up.wait()
    for part, cols in tiles(gate_ref.shape[1]):
        up_act = from_rows(part, up, cols)
        hidden[part, cols] = (gated[part, cols] * up_act).astype(hidden.dtype)
    fetch_down.wait()
    first = 0
    for out_ref in out_refs:
        for part, cols in tiles(out_ref.shape[1]):
            weights = down[:, pl.ds(first + cols.start, step)]
            out_ref[part, cols] = product(hidden[part, :], weights).astype(out_ref.dtype)
        first += out_ref.shape[1]


def expert_ffn(rows, gate_mat, up_mat, down_mat, pieces):
    count = rows[0].shape[0]
    width, ff = gate_mat.shape
    whole = pl.BlockSpec(memory_space=pltpu.VMEM)
    away = pl.BlockSpec(memory_space=pltpu.HBM)
    return pl.pallas_call(
        lambda *refs: ffn_kernel(256, len(rows), *refs),
        out_shape=[jax.ShapeDtypeStruct((count, piece), jnp.bfloat16) for piece in pieces],
        in_specs=[whole] * (len(rows) + 1) + [away, away],
        out_specs=[whole] * len(pieces),
        scratch_shapes=[
            pltpu.VMEM((width, ff), jnp.bfloat16),
            pltpu.VMEM((ff, width), jnp.bfloat16),
            pltpu.VMEM((count, ff), jnp.float32),
            pltpu.VMEM((count, ff), jnp.bfloat16),
            pltpu.SemaphoreType.DMA((2,)),
        ],
        compiler_params=pltpu.CompilerParams(vmem_limit_bytes=44 * MIB),
        cost_estimate=pl.CostEstimate(
            flops=6 * count * width * ff,
            bytes_accessed=6 * width * ff + 4 * count * width,
            transcendentals=count * ff,
        ),
        name=f"ffn_{len(rows)}_{len(pieces)}",
    )(*rows, gate_mat, up_mat, down_mat)


def combine_kernel(map_ref, *refs):
    results_refs, out_ref = refs[:-1], refs[-1]
    first = 0
    for results_ref in results_refs:
        width = results_ref.shape[1]
        out_ref[:, pl.ds(first, width)] = lax.dot_general(
            map_ref[...],
            results_ref[...],
            (((0,), (0,)), ((), ())),
            preferred_element_type=jnp.float32,
        ).astype(out_ref.dtype)
        first += width


def combine(combine_map, results):
    whole = pl.BlockSpec(memory_space=pltpu.VMEM)
    width = sum(result.shape[1] for result in results)
    return pl.pallas_call(
        combine_kernel,
        out_shape=jax.ShapeDtypeStruct((combine_map.shape[1], width), jnp.bfloat16),
        in_specs=[whole] * (len(results) + 1),
        out_specs=whole,
        compiler_params=pltpu.CompilerParams(vmem_limit_bytes=16 * MIB),
        name=f"combine_{len(results)}",
    )(combine_map, *results)


def layer(out_pieces, back_pieces, tokens, expert_ids, gate_fixed, w_gate, w_up, w_down):
    tok_dev, width = tokens.shape
    top_count = expert_ids.shape[1]
    experts = lax.axis_size(("node", "chip")) * w_gate.shape[0]
    capacity = tok_dev * top_count // experts
    outbound, combine_map = build_tables(
        expert_ids, gate_fixed, tokens, experts, capacity, out_pieces
    )

    def exchange(rows):
        blocks = rows.reshape(experts, capacity, rows.shape[1])
        return lax.all_to_all(
            blocks, ("node", "chip"), split_axis=0, concat_axis=0, tiled=True
        ).reshape(rows.shape)

    arrived = [exchange(rows) for rows in outbound]
    served = expert_ffn(arrived, w_gate[0], w_up[0], w_down[0], back_pieces)
    return combine(combine_map, [exchange(rows) for rows in served])


def on_device(*args):
    return lax.cond(
        lax.axis_index("dp") % 2 == 0,
        lambda *a: layer(*PIECES[0], *a),
        lambda *a: layer(*PIECES[1], *a),
        *args,
    )


def solution(mesh):
    return jax.shard_map(
        on_device,
        mesh=mesh,
        in_specs=(
            P(("dp", "node", "chip"), None),
            P(("dp", "node", "chip"), None),
            P(("dp", "node", "chip"), None),
            P(("node", "chip"), None, None),
            P(("node", "chip"), None, None),
            P(("node", "chip"), None, None),
        ),
        out_specs=P(("dp", "node", "chip"), None),
        check_vma=False,
    )
```

```python
import jax
import jax.numpy as jnp
from jax import lax
from jax.experimental import pallas as pl
from jax.experimental.pallas import tpu as pltpu
from jax.sharding import PartitionSpec as P

MIB = 1024 * 1024
TILE = 128
PIECES = (((2048,), (2048,)), ((128, 256, 1664), (2048,)))


def tables_kernel(experts, pieces, ids_ref, gates_ref, tokens_ref, *refs):
    rows_refs, map_ref = refs[: len(pieces)], refs[len(pieces)]
    ids_here, gates_here, tokens, rows, combine_map, arrived, left = refs[len(pieces) + 1 :]
    fetch_ids = pltpu.make_async_copy(ids_ref, ids_here, arrived.at[0])
    fetch_gates = pltpu.make_async_copy(gates_ref, gates_here, arrived.at[1])
    fetch_tokens = pltpu.make_async_copy(tokens_ref, tokens, arrived.at[2])
    fetch_ids.start()
    fetch_gates.start()
    fetch_tokens.start()
    top_count, tok_dev = ids_ref.shape
    slots = rows.shape[0]
    capacity = slots // experts
    row = lax.broadcasted_iota(jnp.int32, (slots, experts), 0)
    spread = jnp.where(
        row // capacity == lax.broadcasted_iota(jnp.int32, (slots, experts), 1), 1.0, 0.0
    ).astype(jnp.bfloat16)
    slot = lax.broadcasted_iota(jnp.int32, (slots, tok_dev), 0) % capacity
    earlier = lax.broadcasted_iota(jnp.int32, (tok_dev, tok_dev), 0) < lax.broadcasted_iota(
        jnp.int32, (tok_dev, tok_dev), 1
    )
    expert = lax.broadcasted_iota(jnp.int32, (experts, tok_dev), 0)
    fetch_ids.wait()
    ids = ids_here[...]
    named = jnp.zeros((experts, tok_dev), jnp.float32)
    for k in range(top_count):
        named = jnp.where(ids[k : k + 1, :] == expert, 1.0, named)
    rank = jnp.dot(
        named.astype(jnp.bfloat16),
        jnp.where(earlier, 1.0, 0.0).astype(jnp.bfloat16),
        preferred_element_type=jnp.float32,
    )
    rank = jnp.where(named > 0.0, rank, -1.0).astype(jnp.bfloat16)
    placed = jnp.dot(spread, rank, preferred_element_type=jnp.float32) == slot.astype(
        jnp.float32
    )
    chosen = jnp.where(placed, 1.0, 0.0).astype(jnp.bfloat16)
    fetch_tokens.wait()
    stores = []
    first = 0
    for width, rows_ref in zip(pieces, rows_refs):
        for at in range(0, width, TILE):
            part = pl.ds(first + at, TILE)
            rows[:, part] = jnp.dot(
                chosen, tokens[:, part], preferred_element_type=jnp.float32
            ).astype(rows.dtype)
            stores.append(
                pltpu.make_async_copy(
                    rows.at[:, part], rows_ref.at[:, pl.ds(at, TILE)], left.at[len(stores)]
                )
            )
            stores[-1].start()
        first += width
    fetch_gates.wait()
    gates = gates_here[...].astype(jnp.float32)
    weight = jnp.zeros((experts, tok_dev), jnp.float32)
    for k in range(top_count):
        weight = jnp.where(ids[k : k + 1, :] == expert, gates[k : k + 1, :], weight)
    share = jnp.dot(spread, weight.astype(jnp.bfloat16), preferred_element_type=jnp.float32)
    combine_map[...] = jnp.where(placed, share * (1.0 / 256.0), 0.0).astype(combine_map.dtype)
    stores.append(pltpu.make_async_copy(combine_map, map_ref, left.at[len(stores)]))
    stores[-1].start()
    for store in stores:
        store.wait()


def build_tables(ids, gates, tokens, experts, capacity, pieces):
    tok_dev, width = tokens.shape
    slots = experts * capacity
    away = pl.BlockSpec(memory_space=pltpu.HBM)
    outs = pl.pallas_call(
        lambda *refs: tables_kernel(experts, pieces, *refs),
        out_shape=[jax.ShapeDtypeStruct((slots, piece), jnp.bfloat16) for piece in pieces]
        + [jax.ShapeDtypeStruct((slots, tok_dev), jnp.bfloat16)],
        in_specs=[away] * 3,
        out_specs=[away] * (len(pieces) + 1),
        scratch_shapes=[
            pltpu.VMEM(ids.T.shape, jnp.int32),
            pltpu.VMEM(gates.T.shape, jnp.int32),
            pltpu.VMEM((tok_dev, width), jnp.bfloat16),
            pltpu.VMEM((slots, width), jnp.bfloat16),
            pltpu.VMEM((slots, tok_dev), jnp.bfloat16),
            pltpu.SemaphoreType.DMA((3,)),
            pltpu.SemaphoreType.DMA((width // TILE + 1,)),
        ],
        compiler_params=pltpu.CompilerParams(vmem_limit_bytes=56 * MIB),
        name=f"tables_{len(pieces)}",
    )(ids.T, gates.T, tokens)
    return outs[:-1], outs[-1]


def ffn_kernel(step, count, *refs):
    rows_refs, (gate_ref, up_ref, down_ref), out_refs = refs[:count], refs[count : count + 3], refs[count + 3 : -5]
    up, down, gated, hidden, arrived = refs[-5:]
    fetch_up = pltpu.make_async_copy(up_ref, up, arrived.at[0])
    fetch_down = pltpu.make_async_copy(down_ref, down, arrived.at[1])
    fetch_up.start()
    fetch_down.start()

    def tiles(columns):
        for at in range(0, columns, step):
            for top in range(0, hidden.shape[0], step):
                yield pl.ds(top, step), pl.ds(at, step)

    def product(left, right):
        return jnp.dot(left, right, preferred_element_type=jnp.float32)

    def from_rows(part, weight_ref, cols):
        total, first = None, 0
        for rows_ref in rows_refs:
            depth = rows_ref.shape[1]
            term = product(rows_ref[part, :], weight_ref[pl.ds(first, depth), cols])
            total = term if total is None else total + term
            first += depth
        return total

    for part, cols in tiles(gate_ref.shape[1]):
        gate_act = from_rows(part, gate_ref, cols)
        gated[part, cols] = gate_act / (1.0 + jnp.exp(-gate_act))
    fetch_up.wait()
    for part, cols in tiles(gate_ref.shape[1]):
        up_act = from_rows(part, up, cols)
        hidden[part, cols] = (gated[part, cols] * up_act).astype(hidden.dtype)
    fetch_down.wait()
    first = 0
    for out_ref in out_refs:
        for part, cols in tiles(out_ref.shape[1]):
            weights = down[:, pl.ds(first + cols.start, step)]
            out_ref[part, cols] = product(hidden[part, :], weights).astype(out_ref.dtype)
        first += out_ref.shape[1]


def expert_ffn(rows, gate_mat, up_mat, down_mat, pieces):
    count = rows[0].shape[0]
    width, ff = gate_mat.shape
    whole = pl.BlockSpec(memory_space=pltpu.VMEM)
    away = pl.BlockSpec(memory_space=pltpu.HBM)
    return pl.pallas_call(
        lambda *refs: ffn_kernel(256, len(rows), *refs),
        out_shape=[jax.ShapeDtypeStruct((count, piece), jnp.bfloat16) for piece in pieces],
        in_specs=[whole] * (len(rows) + 1) + [away, away],
        out_specs=[whole] * len(pieces),
        scratch_shapes=[
            pltpu.VMEM((width, ff), jnp.bfloat16),
            pltpu.VMEM((ff, width), jnp.bfloat16),
            pltpu.VMEM((count, ff), jnp.float32),
            pltpu.VMEM((count, ff), jnp.bfloat16),
            pltpu.SemaphoreType.DMA((2,)),
        ],
        compiler_params=pltpu.CompilerParams(vmem_limit_bytes=44 * MIB),
        cost_estimate=pl.CostEstimate(
            flops=6 * count * width * ff,
            bytes_accessed=6 * width * ff + 4 * count * width,
            transcendentals=count * ff,
        ),
        name=f"ffn_{len(rows)}_{len(pieces)}",
    )(*rows, gate_mat, up_mat, down_mat)


def combine_kernel(map_ref, *refs):
    results_refs, out_ref = refs[:-1], refs[-1]
    first = 0
    for results_ref in results_refs:
        width = results_ref.shape[1]
        out_ref[:, pl.ds(first, width)] = lax.dot_general(
            map_ref[...],
            results_ref[...],
            (((0,), (0,)), ((), ())),
            preferred_element_type=jnp.float32,
        ).astype(out_ref.dtype)
        first += width


def combine(combine_map, results):
    whole = pl.BlockSpec(memory_space=pltpu.VMEM)
    width = sum(result.shape[1] for result in results)
    return pl.pallas_call(
        combine_kernel,
        out_shape=jax.ShapeDtypeStruct((combine_map.shape[1], width), jnp.bfloat16),
        in_specs=[whole] * (len(results) + 1),
        out_specs=whole,
        compiler_params=pltpu.CompilerParams(vmem_limit_bytes=16 * MIB),
        name=f"combine_{len(results)}",
    )(combine_map, *results)


def layer(out_pieces, back_pieces, tokens, expert_ids, gate_fixed, w_gate, w_up, w_down):
    tok_dev, width = tokens.shape
    top_count = expert_ids.shape[1]
    experts = lax.axis_size(("node", "chip")) * w_gate.shape[0]
    capacity = tok_dev * top_count // experts
    outbound, combine_map = build_tables(
        expert_ids, gate_fixed, tokens, experts, capacity, out_pieces
    )

    def exchange(rows):
        blocks = rows.reshape(experts, capacity, rows.shape[1])
        return lax.all_to_all(
            blocks, ("node", "chip"), split_axis=0, concat_axis=0, tiled=True
        ).reshape(rows.shape)

    arrived = [exchange(rows) for rows in outbound]
    served = expert_ffn(arrived, w_gate[0], w_up[0], w_down[0], back_pieces)
    return combine(combine_map, [exchange(rows) for rows in served])


def on_device(*args):
    return lax.cond(
        lax.axis_index("dp") % 2 == 0,
        lambda *a: layer(*PIECES[0], *a),
        lambda *a: layer(*PIECES[1], *a),
        *args,
    )


def solution(mesh):
    return jax.shard_map(
        on_device,
        mesh=mesh,
        in_specs=(
            P(("dp", "node", "chip"), None),
            P(("dp", "node", "chip"), None),
            P(("dp", "node", "chip"), None),
            P(("node", "chip"), None, None),
            P(("node", "chip"), None, None),
            P(("node", "chip"), None, None),
        ),
        out_specs=P(("dp", "node", "chip"), None),
        check_vma=False,
    )
```

```python
import jax
import jax.numpy as jnp
from jax import lax
from jax.experimental import pallas as pl
from jax.experimental.pallas import tpu as pltpu
from jax.sharding import PartitionSpec as P

MIB = 1024 * 1024
TILE = 128
PIECES = (((2048,), (1024, 1024)), ((128, 128, 1792), (2048,)))


def tables_kernel(experts, pieces, ids_ref, gates_ref, tokens_ref, *refs):
    rows_refs, map_ref = refs[: len(pieces)], refs[len(pieces)]
    ids_here, gates_here, tokens, rows, combine_map, arrived, left = refs[len(pieces) + 1 :]
    fetch_ids = pltpu.make_async_copy(ids_ref, ids_here, arrived.at[0])
    fetch_gates = pltpu.make_async_copy(gates_ref, gates_here, arrived.at[1])
    fetch_tokens = pltpu.make_async_copy(tokens_ref, tokens, arrived.at[2])
    fetch_ids.start()
    fetch_gates.start()
    fetch_tokens.start()
    top_count, tok_dev = ids_ref.shape
    slots = rows.shape[0]
    capacity = slots // experts
    row = lax.broadcasted_iota(jnp.int32, (slots, experts), 0)
    spread = jnp.where(
        row // capacity == lax.broadcasted_iota(jnp.int32, (slots, experts), 1), 1.0, 0.0
    ).astype(jnp.bfloat16)
    slot = lax.broadcasted_iota(jnp.int32, (slots, tok_dev), 0) % capacity
    earlier = lax.broadcasted_iota(jnp.int32, (tok_dev, tok_dev), 0) < lax.broadcasted_iota(
        jnp.int32, (tok_dev, tok_dev), 1
    )
    expert = lax.broadcasted_iota(jnp.int32, (experts, tok_dev), 0)
    fetch_ids.wait()
    ids = ids_here[...]
    named = jnp.zeros((experts, tok_dev), jnp.float32)
    for k in range(top_count):
        named = jnp.where(ids[k : k + 1, :] == expert, 1.0, named)
    rank = jnp.dot(
        named.astype(jnp.bfloat16),
        jnp.where(earlier, 1.0, 0.0).astype(jnp.bfloat16),
        preferred_element_type=jnp.float32,
    )
    rank = jnp.where(named > 0.0, rank, -1.0).astype(jnp.bfloat16)
    placed = jnp.dot(spread, rank, preferred_element_type=jnp.float32) == slot.astype(
        jnp.float32
    )
    chosen = jnp.where(placed, 1.0, 0.0).astype(jnp.bfloat16)
    fetch_tokens.wait()
    stores = []
    first = 0
    for width, rows_ref in zip(pieces, rows_refs):
        for at in range(0, width, TILE):
            part = pl.ds(first + at, TILE)
            rows[:, part] = jnp.dot(
                chosen, tokens[:, part], preferred_element_type=jnp.float32
            ).astype(rows.dtype)
            stores.append(
                pltpu.make_async_copy(
                    rows.at[:, part], rows_ref.at[:, pl.ds(at, TILE)], left.at[len(stores)]
                )
            )
            stores[-1].start()
        first += width
    fetch_gates.wait()
    gates = gates_here[...].astype(jnp.float32)
    weight = jnp.zeros((experts, tok_dev), jnp.float32)
    for k in range(top_count):
        weight = jnp.where(ids[k : k + 1, :] == expert, gates[k : k + 1, :], weight)
    share = jnp.dot(spread, weight.astype(jnp.bfloat16), preferred_element_type=jnp.float32)
    combine_map[...] = jnp.where(placed, share * (1.0 / 256.0), 0.0).astype(combine_map.dtype)
    stores.append(pltpu.make_async_copy(combine_map, map_ref, left.at[len(stores)]))
    stores[-1].start()
    for store in stores:
        store.wait()


def build_tables(ids, gates, tokens, experts, capacity, pieces):
    tok_dev, width = tokens.shape
    slots = experts * capacity
    away = pl.BlockSpec(memory_space=pltpu.HBM)
    outs = pl.pallas_call(
        lambda *refs: tables_kernel(experts, pieces, *refs),
        out_shape=[jax.ShapeDtypeStruct((slots, piece), jnp.bfloat16) for piece in pieces]
        + [jax.ShapeDtypeStruct((slots, tok_dev), jnp.bfloat16)],
        in_specs=[away] * 3,
        out_specs=[away] * (len(pieces) + 1),
        scratch_shapes=[
            pltpu.VMEM(ids.T.shape, jnp.int32),
            pltpu.VMEM(gates.T.shape, jnp.int32),
            pltpu.VMEM((tok_dev, width), jnp.bfloat16),
            pltpu.VMEM((slots, width), jnp.bfloat16),
            pltpu.VMEM((slots, tok_dev), jnp.bfloat16),
            pltpu.SemaphoreType.DMA((3,)),
            pltpu.SemaphoreType.DMA((width // TILE + 1,)),
        ],
        compiler_params=pltpu.CompilerParams(vmem_limit_bytes=56 * MIB),
        name=f"tables_{len(pieces)}",
    )(ids.T, gates.T, tokens)
    return outs[:-1], outs[-1]


def ffn_kernel(step, count, *refs):
    rows_refs, (gate_ref, up_ref, down_ref), out_refs = refs[:count], refs[count : count + 3], refs[count + 3 : -5]
    up, down, gated, hidden, arrived = refs[-5:]
    fetch_up = pltpu.make_async_copy(up_ref, up, arrived.at[0])
    fetch_down = pltpu.make_async_copy(down_ref, down, arrived.at[1])
    fetch_up.start()
    fetch_down.start()

    def tiles(columns):
        for at in range(0, columns, step):
            for top in range(0, hidden.shape[0], step):
                yield pl.ds(top, step), pl.ds(at, step)

    def product(left, right):
        return jnp.dot(left, right, preferred_element_type=jnp.float32)

    def from_rows(part, weight_ref, cols):
        total, first = None, 0
        for rows_ref in rows_refs:
            depth = rows_ref.shape[1]
            term = product(rows_ref[part, :], weight_ref[pl.ds(first, depth), cols])
            total = term if total is None else total + term
            first += depth
        return total

    for part, cols in tiles(gate_ref.shape[1]):
        gate_act = from_rows(part, gate_ref, cols)
        gated[part, cols] = gate_act / (1.0 + jnp.exp(-gate_act))
    fetch_up.wait()
    for part, cols in tiles(gate_ref.shape[1]):
        up_act = from_rows(part, up, cols)
        hidden[part, cols] = (gated[part, cols] * up_act).astype(hidden.dtype)
    fetch_down.wait()
    first = 0
    for out_ref in out_refs:
        for part, cols in tiles(out_ref.shape[1]):
            weights = down[:, pl.ds(first + cols.start, step)]
            out_ref[part, cols] = product(hidden[part, :], weights).astype(out_ref.dtype)
        first += out_ref.shape[1]


def expert_ffn(rows, gate_mat, up_mat, down_mat, pieces):
    count = rows[0].shape[0]
    width, ff = gate_mat.shape
    whole = pl.BlockSpec(memory_space=pltpu.VMEM)
    away = pl.BlockSpec(memory_space=pltpu.HBM)
    return pl.pallas_call(
        lambda *refs: ffn_kernel(256, len(rows), *refs),
        out_shape=[jax.ShapeDtypeStruct((count, piece), jnp.bfloat16) for piece in pieces],
        in_specs=[whole] * (len(rows) + 1) + [away, away],
        out_specs=[whole] * len(pieces),
        scratch_shapes=[
            pltpu.VMEM((width, ff), jnp.bfloat16),
            pltpu.VMEM((ff, width), jnp.bfloat16),
            pltpu.VMEM((count, ff), jnp.float32),
            pltpu.VMEM((count, ff), jnp.bfloat16),
            pltpu.SemaphoreType.DMA((2,)),
        ],
        compiler_params=pltpu.CompilerParams(vmem_limit_bytes=44 * MIB),
        cost_estimate=pl.CostEstimate(
            flops=6 * count * width * ff,
            bytes_accessed=6 * width * ff + 4 * count * width,
            transcendentals=count * ff,
        ),
        name=f"ffn_{len(rows)}_{len(pieces)}",
    )(*rows, gate_mat, up_mat, down_mat)


def combine_kernel(map_ref, *refs):
    results_refs, out_ref = refs[:-1], refs[-1]
    first = 0
    for results_ref in results_refs:
        width = results_ref.shape[1]
        out_ref[:, pl.ds(first, width)] = lax.dot_general(
            map_ref[...],
            results_ref[...],
            (((0,), (0,)), ((), ())),
            preferred_element_type=jnp.float32,
        ).astype(out_ref.dtype)
        first += width


def combine(combine_map, results):
    whole = pl.BlockSpec(memory_space=pltpu.VMEM)
    width = sum(result.shape[1] for result in results)
    return pl.pallas_call(
        combine_kernel,
        out_shape=jax.ShapeDtypeStruct((combine_map.shape[1], width), jnp.bfloat16),
        in_specs=[whole] * (len(results) + 1),
        out_specs=whole,
        compiler_params=pltpu.CompilerParams(vmem_limit_bytes=16 * MIB),
        name=f"combine_{len(results)}",
    )(combine_map, *results)


def layer(out_pieces, back_pieces, tokens, expert_ids, gate_fixed, w_gate, w_up, w_down):
    tok_dev, width = tokens.shape
    top_count = expert_ids.shape[1]
    experts = lax.axis_size(("node", "chip")) * w_gate.shape[0]
    capacity = tok_dev * top_count // experts
    outbound, combine_map = build_tables(
        expert_ids, gate_fixed, tokens, experts, capacity, out_pieces
    )

    def exchange(rows):
        blocks = rows.reshape(experts, capacity, rows.shape[1])
        return lax.all_to_all(
            blocks, ("node", "chip"), split_axis=0, concat_axis=0, tiled=True
        ).reshape(rows.shape)

    arrived = [exchange(rows) for rows in outbound]
    served = expert_ffn(arrived, w_gate[0], w_up[0], w_down[0], back_pieces)
    return combine(combine_map, [exchange(rows) for rows in served])


def on_device(*args):
    return lax.cond(
        lax.axis_index("dp") % 2 == 0,
        lambda *a: layer(*PIECES[0], *a),
        lambda *a: layer(*PIECES[1], *a),
        *args,
    )


def solution(mesh):
    return jax.shard_map(
        on_device,
        mesh=mesh,
        in_specs=(
            P(("dp", "node", "chip"), None),
            P(("dp", "node", "chip"), None),
            P(("dp", "node", "chip"), None),
            P(("node", "chip"), None, None),
            P(("node", "chip"), None, None),
            P(("node", "chip"), None, None),
        ),
        out_specs=P(("dp", "node", "chip"), None),
        check_vma=False,
    )
```
